32 devices in a mesh: section: 16 (over z, x, core), tensor: 2 (over y).
Axes of the slice: x: 2, y: 2, z: 4, core: 2. Of those that a mesh axis runs over, the one named last changes fastest.
Arguments:
- queries: bfloat16 [2, 16, 4, 128, 3072], P(None, 'section', None, None, 'tensor'), may hold values from -6 to 6
- enc_keys: bfloat16 [2, 16, 4, 128, 3072], P(None, 'section', None, None, 'tensor'), may hold values from -6 to 6
- enc_values: bfloat16 [2, 16, 4, 128, 3072], P(None, 'section', None, None, 'tensor'), may hold values from -6 to 6
- w_query: bfloat16 [2, 16, 3072, 3072], P(None, 'section', None, 'tensor'), may hold values from -0.109375 to 0.109375
- w_out: bfloat16 [2, 16, 3072, 3072], P(None, 'section', 'tensor'), may hold values from -0.109375 to 0.109375
- arriving: bfloat16 [2, 16, 3072, 128], P(None, 'section', 'tensor'), may hold values from -6 to 6
- loss_grad: bfloat16 [2, 3, 3072, 128], P(None, None, 'tensor'), may hold values from -6 to 6
- dec_lengths: int32 [2, 16, 4, 4], P(None, 'section'), may hold values from 1 to 64, 128 in all within a row
- enc_lengths: int32 [2, 16, 4, 4], P(None, 'section'), may hold values from 1 to 64, 128 in all within a row
Outputs:
- grads: bfloat16 [2, 16, 4, 3072, 128], P(None, 'section', None, 'tensor')
The draws below stay inside these ranges and needn't reach their ends.
Inputs may be any that keep to these rules, and one draw needn't show every extreme that they name: `dec_lengths`: each row of 4 lengths sums to 128, and its largest is 64. `enc_lengths`: each row of 4 lengths sums to 128, and its largest is 64.
All inputs are finite; a program needn't handle non-finite values.
Results may differ from the reference program's by a relative error of at most 0.012.
Values may be sent and summed in bfloat16 or wider, within the bound.
A program may use at most 192 MiB of HBM per device.

```python
import math
import jax
import jax.numpy as jnp
import numpy as np
from jax import lax

WIDTH = 3072
HEADS = 24
HEAD = 128
INNER = 3072
SEQ = 128
DOCS = 4
TICKS = 4
MOST = 64
SECTIONS = 16
N_TENSOR = 2


def draw_queries(key, part):
    key = jax.random.fold_in(key, 41)
    drawn = jax.random.normal(key, (2, SECTIONS, TICKS, SEQ, HEADS * HEAD), jnp.float32)
    return jnp.clip(drawn, -6.0, 6.0).astype(jnp.bfloat16)


def draw_enc_keys(key, part):
    key = jax.random.fold_in(key, 43)
    drawn = jax.random.normal(key, (2, SECTIONS, TICKS, SEQ, HEADS * HEAD), jnp.float32)
    return jnp.clip(drawn, -6.0, 6.0).astype(jnp.bfloat16)


def block_scale(key, dims, split, low, largest):
    gain = 1.0
    for dim, blocks in split:
        steps = jax.random.uniform(jax.random.fold_in(jax.random.fold_in(key, 6), dim), (blocks,), jnp.float32, low / len(split), largest / len(split))
        gain = gain * jnp.repeat(jnp.exp(steps), dims[dim] // blocks).reshape((-1,) + (1,) * (len(dims) - 1 - dim))
    return gain


def length_profile(count, total, reach, skew):
    weights = [(1 << 20) // math.isqrt(standing ** skew) + 1 for standing in range(2, count + 1)]
    rest, holding = total - reach - (count - 1), [1] * (count - 1)
    while rest > 0:
        free = [i for i in range(count - 1) if holding[i] < reach]
        mass, left = sum([weights[i] for i in free]), rest
        for i in free:
            addition = min(reach - holding[i], max(1, left * weights[i] // mass), rest)
            holding[i] = holding[i] + addition
            rest = rest - addition
    return np.array([reach] + holding)


def ragged_sizes(key, amount, total, reach, lean):
    if amount == 2:
        one = jax.random.randint(key, (), max(1, total - reach), min(reach, total - 1) + 1)
        return jnp.stack([one, total - one])
    sizes = jnp.asarray(length_profile(amount, total, reach, lean), jnp.int32)
    pairs = (amount - 1) // 2
    giver, taker = sizes[1:1 + 2 * pairs:2], sizes[2:2 + 2 * pairs:2]
    margin = jnp.minimum(giver - 1, reach - taker)
    shifted = jax.random.randint(jax.random.fold_in(key, 1), (pairs,), 0, 1 << 20) % (margin + 1)
    sizes = sizes.at[1:1 + 2 * pairs:2].set(giver - shifted).at[2:2 + 2 * pairs:2].set(taker + shifted)
    return sizes[jax.random.permutation(jax.random.fold_in(key, 2), amount)]


def noise(stream_key, extent, deviation, bound, cuts=(), held_as=jnp.bfloat16):
    values = deviation * jax.random.normal(stream_key, extent, jnp.float32)
    if cuts:
        values = values * block_scale(stream_key, extent, cuts, -0.22, 0.18)
    return jnp.clip(values, -bound, bound).astype(held_as)


def setup_inputs(seed: int = 0) -> dict:
    keys = jax.random.split(jax.random.key(seed), 10)
    queries = draw_queries(jax.random.fold_in(keys[9], 71), 0)
    enc_keys = draw_enc_keys(jax.random.fold_in(keys[9], 71), 0)
    enc_values = noise(keys[2], (2, SECTIONS, TICKS, SEQ, INNER), 1.0, 6.0, ((1, 16), (4, 2)))
    w_query = noise(keys[3], (2, SECTIONS, WIDTH, INNER), WIDTH ** -0.5, 0.109375, ((1, 16), (3, 2)))
    w_out = noise(keys[4], (2, SECTIONS, INNER, WIDTH), INNER ** -0.5, 0.109375, ((1, 16), (2, 2)))
    arriving = noise(keys[5], (2, SECTIONS, WIDTH, SEQ), 1.0, 6.0, ((1, 16), (2, 2)))
    loss_grad = noise(keys[6], (2, TICKS - 1, WIDTH, SEQ), 1.0, 6.0, ((2, 2),))
    dec_lengths = jax.vmap(lambda own: ragged_sizes(own, DOCS, SEQ, MOST, 1))(jax.random.split(keys[7], 2 * SECTIONS * TICKS)).reshape((2, SECTIONS, TICKS, DOCS)).astype(jnp.int32)
    enc_lengths = jax.vmap(lambda own: ragged_sizes(own, DOCS, SEQ, MOST, 1))(jax.random.split(keys[8], 2 * SECTIONS * TICKS)).reshape((2, SECTIONS, TICKS, DOCS)).astype(jnp.int32)
    return {"queries": queries, "enc_keys": enc_keys, "enc_values": enc_values, "w_query": w_query, "w_out": w_out, "arriving": arriving, "loss_grad": loss_grad, "dec_lengths": dec_lengths, "enc_lengths": enc_lengths}


def doc_ids(lengths):
    starts = jnp.cumsum(lengths) - lengths
    places = jnp.arange(SEQ, dtype=jnp.int32)
    return lax.optimization_barrier(jnp.sum((places[:, None] >= starts[None, 1:]).astype(jnp.int32), axis=1))

def layer_grad(operands):
    entering, queries, enc_keys, enc_values, w_query, w_out, dec_len, enc_len = operands
    attn_grad = jnp.dot(w_out, entering, preferred_element_type=jnp.float32).astype(jnp.bfloat16)
    allowed = doc_ids(dec_len)[:, None] == doc_ids(enc_len)[None, :]
    q_heads = queries.astype(jnp.float32).reshape(SEQ, HEADS, HEAD)
    k_heads = enc_keys.astype(jnp.float32).reshape(SEQ, HEADS, HEAD)
    v_heads = enc_values.astype(jnp.float32).reshape(SEQ, HEADS, HEAD)
    scores = jnp.einsum('phe,jhe->hpj', q_heads, k_heads) * HEAD ** (-0.5)
    scores = jnp.where(allowed[None], scores, -1e+30)
    row_top = lax.optimization_barrier(jnp.max(scores, axis=2, keepdims=True))
    weights = jnp.exp(scores - row_top)
    weights = weights / lax.optimization_barrier(jnp.sum(weights, axis=2, keepdims=True))
    grad_heads = attn_grad.astype(jnp.float32).reshape(HEADS, HEAD, SEQ)
    prob_grad = jnp.einsum('hep,jhe->hpj', grad_heads, v_heads)
    rowdot = lax.optimization_barrier(jnp.sum(weights * prob_grad, axis=2, keepdims=True))
    score_grad = (weights * (prob_grad - rowdot)).astype(jnp.bfloat16)
    dquery = (jnp.einsum('hpj,jhe->phe', score_grad.astype(jnp.float32), k_heads) * HEAD ** (-0.5)).astype(jnp.bfloat16)
    groups = dquery.astype(jnp.float32).reshape(SEQ, N_TENSOR, INNER // N_TENSOR)
    w_groups = w_query.astype(jnp.float32).reshape(WIDTH, N_TENSOR, INNER // N_TENSOR)
    partials = jnp.einsum('dgc,pgc->gdp', w_groups, groups)
    partials = lax.optimization_barrier(partials.astype(jnp.bfloat16)).astype(jnp.float32)
    return (entering.astype(jnp.float32) + lax.optimization_barrier(jnp.sum(partials, axis=0))).astype(jnp.bfloat16)

def merge_lead(array):
    return array.reshape((2 * SECTIONS,) + array.shape[2:])

def reference(queries, enc_keys, enc_values, w_query, w_out, arriving, loss_grad, dec_lengths, enc_lengths):
    current = arriving
    history = []
    for tick_index in range(TICKS):
        if tick_index > 0:
            down_grad = jnp.concatenate([current[0, 1:], loss_grad[0, tick_index - 1][None]], axis=0)
            up_grad = jnp.concatenate([loss_grad[1, tick_index - 1][None], current[1, :-1]], axis=0)
            current = jnp.stack([down_grad, up_grad])
        operands = (merge_lead(current), merge_lead(queries[:, :, tick_index]), merge_lead(enc_keys[:, :, tick_index]), merge_lead(enc_values[:, :, tick_index]), merge_lead(w_query), merge_lead(w_out), merge_lead(dec_lengths[:, :, tick_index]), merge_lead(enc_lengths[:, :, tick_index]))
        current = lax.map(layer_grad, operands).reshape(current.shape)
        history.append(current)
    return jnp.stack(history, axis=2)
```

```python
import functools

import jax
import jax.numpy as jnp
from jax import lax
from jax.experimental import pallas as pl
from jax.experimental.pallas import tpu as pltpu
from jax.sharding import PartitionSpec as P

HEAD = 128
CHUNK = 384
MESH = pl.DeviceIdType.MESH


def largest_divisor(total, limit):
    return max(size for size in range(1, min(total, limit) + 1) if total % size == 0)


def relay_kernel(
    sections, group, dims,
    dec_ref, enc_ref, q_hbm, k_hbm, v_hbm, wq_hbm, wo_hbm, arriving_ref, loss_ref,
    out_ref,
    wq, wo, qs, ks, vs, entering, attn, dqt, part, landed,
    wq_sem, wo_sem, qkv_sem, enter_sem, feed_send, next_send, rs_send, rs_recv,
):
    ticks, seq, inner, width, rows, chunk = dims
    chunks = rows // chunk
    section = lax.axis_index("section")
    me = lax.axis_index("tensor")

    def peer(step):
        return lax.rem(me + step, group)

    def load_qkv(c, t):
        return [
            pltpu.make_async_copy(hbm.at[c, t], vmem.at[c], qkv_sem.at[c, which])
            for which, (hbm, vmem) in enumerate(((q_hbm, qs), (k_hbm, ks), (v_hbm, vs)))
        ]

    def load_wo(c):
        return pltpu.make_async_copy(wo_hbm.at[c], wo.at[c], wo_sem.at[c])

    def load_wq(c):
        return pltpu.make_async_copy(wq_hbm.at[c], wq.at[c], wq_sem.at[c])

    for c in range(2):
        load_wo(c).start()
        for copy in load_qkv(c, 0):
            copy.start()
        load_wq(c).start()

    barrier = pltpu.get_barrier_semaphore()
    for step in range(1, group):
        pl.semaphore_signal(
            barrier, inc=1, device_id=(section, peer(step)), device_id_type=MESH
        )

    @pl.when(section > 0)
    def _():
        for step in range(group):
            pl.semaphore_signal(
                barrier, inc=1, device_id=(section - 1, peer(step)), device_id_type=MESH
            )

    @pl.when(section < sections - 1)
    def _():
        for step in range(group):
            pl.semaphore_signal(
                barrier, inc=1, device_id=(section + 1, peer(step)), device_id_type=MESH
            )

    around = (section > 0).astype(jnp.int32) + (section < sections - 1).astype(jnp.int32)
    pl.semaphore_wait(barrier, group - 1 + group * around)

    def place(source, k):
        return pl.ds(pl.multiple_of(source * rows + k * chunk, chunk), chunk)

    def here(k):
        return pl.ds(pl.multiple_of(k * chunk, chunk), chunk)

    def feed_copy(source, c, t, k, step):
        return pltpu.make_async_remote_copy(
            src_ref=source,
            dst_ref=entering.at[t, c, place(me, k)],
            send_sem=feed_send.at[t, c, k, step],
            recv_sem=enter_sem.at[t, c, k, me],
            device_id=(section, peer(step)),
            device_id_type=MESH,
        )

    def feed(source, c, t, k):
        for step in range(1, group):
            feed_copy(source, c, t, k, step).start()
        pltpu.make_async_copy(
            source, entering.at[t, c, place(me, k)], enter_sem.at[t, c, k, me]
        ).start()

    def next_copy(c, t, k, step):
        return pltpu.make_async_remote_copy(
            src_ref=out_ref.at[c, t, here(k)],
            dst_ref=entering.at[t + 1, c, place(me, k)],
            send_sem=next_send.at[t, c, k, step],
            recv_sem=enter_sem.at[t + 1, c, k, me],
            device_id=(section + 2 * c - 1, peer(step)),
            device_id_type=MESH,
        )

    def reduce_copy(c, t, k, step):
        return pltpu.make_async_remote_copy(
            src_ref=part.at[c, place(peer(step), k)],
            dst_ref=landed.at[t, c, step - 1, here(k)],
            send_sem=rs_send.at[t, c, k, step - 1],
            recv_sem=rs_recv.at[t, c, k, step - 1],
            device_id=(section, peer(step)),
            device_id_type=MESH,
        )

    def goes_on(c, t):
        target = section + 2 * c - 1
        return (target >= 0) & (target < sections) & (t + 1 < ticks)

    def begins(c, t):
        origin = section - 2 * c + 1
        return ((origin < 0) | (origin >= sections)) & (t + 1 < ticks)

    for c in range(2):
        for k in range(chunks):
            feed(arriving_ref.at[c, here(k)], c, 0, k)

    def finish(c, t, k):
        total = (
            entering[t, c, place(me, k), :].astype(jnp.float32)
            + part[c, place(me, k), :].astype(jnp.float32)
        )
        for step in range(1, group):
            copy = reduce_copy(c, t, k, step)
            copy.wait_send()
            copy.wait_recv()
            total += landed[t, c, step - 1, here(k), :].astype(jnp.float32)
        out_ref[c, t, here(k), :] = total.astype(jnp.bfloat16)

        @pl.when(goes_on(c, t))
        def _():
            for step in list(range(1, group)) + [0]:
                next_copy(c, t, k, step).start()

        @pl.when(begins(c, t))
        def _():
            feed(loss_ref.at[c, jnp.minimum(t, ticks - 2), here(k)], c, t + 1, k)

    tile = largest_divisor(inner, 384)
    heads = inner // HEAD
    unroll = largest_divisor(heads, 4)

    def doc_ids(lens, base, axis):
        places = lax.broadcasted_iota(jnp.int32, (seq, seq), axis)
        first = lens[base]
        second = first + lens[base + 1]
        third = second + lens[base + 2]
        return (
            (places >= first).astype(jnp.int32)
            + (places >= second).astype(jnp.int32)
            + (places >= third).astype(jnp.int32)
        )

    def phase(index, carry):
        c = lax.rem(index, 2)
        t = index // 2
        for k in range(chunks):
            for source in range(group):
                pltpu.make_async_copy(
                    entering.at[t, c, place(source, k)],
                    entering.at[t, c, place(source, k)],
                    enter_sem.at[t, c, k, source],
                ).wait()

        @pl.when(t == 0)
        def _():
            load_wo(c).wait()

        def out_tile(r, carry):
            span = pl.ds(pl.multiple_of(r * tile, tile), tile)
            attn[span, :] = jnp.dot(
                wo[c, span, :], entering[t, c], preferred_element_type=jnp.float32
            ).astype(jnp.bfloat16)
            return carry

        lax.fori_loop(0, inner // tile, out_tile, 0)
        for copy in load_qkv(c, t):
            copy.wait()
        base = (c * ticks + t) * 4
        allowed = doc_ids(enc_ref, base, 0) == doc_ids(dec_ref, base, 1)

        def head_group(g, carry):
            for within in range(unroll):
                span = pl.ds(pl.multiple_of((g * unroll + within) * HEAD, HEAD), HEAD)
                key = ks[c, :, span]
                scores = lax.dot_general(
                    key, qs[c, :, span], (((1,), (1,)), ((), ())),
                    preferred_element_type=jnp.float32,
                ) * HEAD ** (-0.5)
                scores = jnp.where(allowed, scores, -1e30)
                top = jnp.max(scores, axis=0, keepdims=True)
                weights = jnp.exp(scores - top)
                weights = weights * (1.0 / jnp.sum(weights, axis=0, keepdims=True))
                prob_grad = jnp.dot(
                    vs[c, :, span], attn[span, :], preferred_element_type=jnp.float32
                )
                rowdot = jnp.sum(weights * prob_grad, axis=0, keepdims=True)
                score_grad = (weights * (prob_grad - rowdot)).astype(jnp.bfloat16)
                dqt[span, :] = (
                    lax.dot_general(
                        key, score_grad, (((0,), (0,)), ((), ())),
                        preferred_element_type=jnp.float32,
                    ) * HEAD ** (-0.5)
                ).astype(jnp.bfloat16)
            return carry

        lax.fori_loop(0, heads // unroll, head_group, 0)

        @pl.when(t + 1 < ticks)
        def _():
            for copy in load_qkv(c, jnp.minimum(t + 1, ticks - 1)):
                copy.start()

        @pl.when(t == 0)
        def _():
            load_wq(c).wait()

        def head_term(source, k):
            span = place(source, k)
            part[c, span, :] = jnp.dot(
                wq[c, span, :], dqt[...], preferred_element_type=jnp.float32
            ).astype(jnp.bfloat16)

        def send_chunk(k, carry):
            @pl.when(index > 0)
            def _():
                before = jnp.maximum(index - 1, 0)
                finish(lax.rem(before, 2), before // 2, k)

            for step in range(1, group):
                head_term(peer(step), k)
                reduce_copy(c, t, k, step).start()
            return carry

        lax.fori_loop(0, chunks, send_chunk, 0)

        def own_chunk(k, carry):
            head_term(me, k)
            return carry

        lax.fori_loop(0, chunks, own_chunk, 0)
        return carry

    lax.fori_loop(0, 2 * ticks, phase, 0)

    def last_chunk(k, carry):
        finish(1, ticks - 1, k)
        return carry

    lax.fori_loop(0, chunks, last_chunk, 0)

    def drain(index, carry):
        c = lax.rem(index, 2)
        t = index // 2

        @pl.when(t == 0)
        def _():
            for k in range(chunks):
                for step in range(1, group):
                    feed_copy(arriving_ref.at[c, here(k)], c, 0, k, step).wait_send()

        @pl.when(goes_on(c, t))
        def _():
            for k in range(chunks):
                for step in range(group):
                    next_copy(c, t, k, step).wait_send()

        @pl.when(begins(c, t))
        def _():
            for k in range(chunks):
                for step in range(1, group):
                    feed_copy(
                        loss_ref.at[c, jnp.minimum(t, ticks - 2), here(k)], c, t + 1, k, step
                    ).wait_send()

        return carry

    lax.fori_loop(0, 2 * ticks, drain, 0)


def local(
    queries, enc_keys, enc_values, w_query, w_out, arriving, loss_grad, dec_lengths, enc_lengths
):
    sections = lax.axis_size("section")
    group = lax.axis_size("tensor")
    _, _, ticks, seq, inner = queries.shape
    width = w_query.shape[2]
    rows = arriving.shape[2]
    chunk = largest_divisor(rows, CHUNK)
    chunks = rows // chunk
    bf16 = jnp.bfloat16
    vmem = pl.BlockSpec(memory_space=pltpu.VMEM)
    smem = pl.BlockSpec(memory_space=pltpu.SMEM)
    anywhere = pl.BlockSpec(memory_space=pl.ANY)
    dma = pltpu.SemaphoreType.DMA
    grads = pl.pallas_call(
        functools.partial(
            relay_kernel, sections, group, (ticks, seq, inner, width, rows, chunk)
        ),
        out_shape=jax.ShapeDtypeStruct((2, ticks, rows, seq), bf16),
        in_specs=[smem, smem] + [anywhere] * 7,
        out_specs=vmem,
        scratch_shapes=[
            pltpu.VMEM((2, width, inner), bf16),
            pltpu.VMEM((2, inner, width), bf16),
            pltpu.VMEM((2, seq, inner), bf16),
            pltpu.VMEM((2, seq, inner), bf16),
            pltpu.VMEM((2, seq, inner), bf16),
            pltpu.VMEM((ticks, 2, width, seq), bf16),
            pltpu.VMEM((inner, seq), bf16),
            pltpu.VMEM((inner, seq), bf16),
            pltpu.VMEM((2, width, seq), bf16),
            pltpu.VMEM((ticks, 2, group - 1, rows, seq), bf16),
            dma((2,)),
            dma((2,)),
            dma((2, 3)),
            dma((ticks, 2, chunks, group)),
            dma((ticks, 2, chunks, group)),
            dma((ticks, 2, chunks, group)),
            dma((ticks, 2, chunks, group - 1)),
            dma((ticks, 2, chunks, group - 1)),
        ],
        compiler_params=pltpu.CompilerParams(
            collective_id=0, has_side_effects=True, vmem_limit_bytes=60 * 1024 * 1024
        ),
        cost_estimate=pl.CostEstimate(
            flops=4 * ticks * inner * (2 * width + 3 * seq) * seq,
            bytes_accessed=2 * (4 * width * inner + 6 * ticks * seq * inner),
            transcendentals=2 * ticks * seq * inner,
        ),
    )(
        dec_lengths.reshape(-1),
        enc_lengths.reshape(-1),
        queries[:, 0],
        enc_keys[:, 0],
        enc_values[:, 0],
        w_query[:, 0],
        w_out[:, 0],
        arriving[:, 0],
        loss_grad,
    )
    return grads[:, None]


def solution(mesh):
    in_specs = (
        P(None, "section", None, None, "tensor"),
        P(None, "section", None, None, "tensor"),
        P(None, "section", None, None, "tensor"),
        P(None, "section", None, "tensor"),
        P(None, "section", "tensor", None),
        P(None, "section", "tensor", None),
        P(None, None, "tensor", None),
        P(None, "section", None, None),
        P(None, "section", None, None),
    )
    out_specs = P(None, "section", None, "tensor", None)
    return jax.shard_map(local, mesh=mesh, in_specs=in_specs, out_specs=out_specs, check_vma=False)
```

```python
import functools

import jax
import jax.numpy as jnp
from jax import lax
from jax.experimental import pallas as pl
from jax.experimental.pallas import tpu as pltpu
from jax.sharding import PartitionSpec as P

HEAD = 128
CHUNK = 768
MESH = pl.DeviceIdType.MESH


def largest_divisor(total, limit):
    return max(size for size in range(1, min(total, limit) + 1) if total % size == 0)


def relay_kernel(
    sections, group, dims,
    dec_ref, enc_ref, q_hbm, k_hbm, v_hbm, wq_hbm, wo_hbm, arriving_ref, loss_ref,
    out_ref,
    wq, wo, qs, ks, vs, entering, attn, dqt, part, landed,
    wq_sem, wo_sem, qkv_sem, enter_sem, feed_send, next_send, rs_send, rs_recv,
):
    ticks, seq, inner, width, rows, chunk = dims
    chunks = rows // chunk
    section = lax.axis_index("section")
    me = lax.axis_index("tensor")

    def peer(step):
        return lax.rem(me + step, group)

    def load_qkv(c, t):
        return [
            pltpu.make_async_copy(hbm.at[c, t], vmem.at[c], qkv_sem.at[c, which])
            for which, (hbm, vmem) in enumerate(((q_hbm, qs), (k_hbm, ks), (v_hbm, vs)))
        ]

    def load_wo(c):
        return pltpu.make_async_copy(wo_hbm.at[c], wo.at[c], wo_sem.at[c])

    def load_wq(c):
        return pltpu.make_async_copy(wq_hbm.at[c], wq.at[c], wq_sem.at[c])

    for c in range(2):
        load_wo(c).start()
        for copy in load_qkv(c, 0):
            copy.start()
        load_wq(c).start()

    barrier = pltpu.get_barrier_semaphore()
    for step in range(1, group):
        pl.semaphore_signal(
            barrier, inc=1, device_id=(section, peer(step)), device_id_type=MESH
        )

    @pl.when(section > 0)
    def _():
        for step in range(group):
            pl.semaphore_signal(
                barrier, inc=1, device_id=(section - 1, peer(step)), device_id_type=MESH
            )

    @pl.when(section < sections - 1)
    def _():
        for step in range(group):
            pl.semaphore_signal(
                barrier, inc=1, device_id=(section + 1, peer(step)), device_id_type=MESH
            )

    around = (section > 0).astype(jnp.int32) + (section < sections - 1).astype(jnp.int32)
    pl.semaphore_wait(barrier, group - 1 + group * around)

    def place(source, k):
        return pl.ds(pl.multiple_of(source * rows + k * chunk, chunk), chunk)

    def here(k):
        return pl.ds(pl.multiple_of(k * chunk, chunk), chunk)

    def feed_copy(source, c, t, k, step):
        return pltpu.make_async_remote_copy(
            src_ref=source,
            dst_ref=entering.at[t, c, place(me, k)],
            send_sem=feed_send.at[t, c, k, step],
            recv_sem=enter_sem.at[t, c, k, me],
            device_id=(section, peer(step)),
            device_id_type=MESH,
        )

    def feed(source, c, t, k):
        for step in range(1, group):
            feed_copy(source, c, t, k, step).start()
        pltpu.make_async_copy(
            source, entering.at[t, c, place(me, k)], enter_sem.at[t, c, k, me]
        ).start()

    def next_copy(c, t, k, step):
        return pltpu.make_async_remote_copy(
            src_ref=out_ref.at[c, t, here(k)],
            dst_ref=entering.at[t + 1, c, place(me, k)],
            send_sem=next_send.at[t, c, k, step],
            recv_sem=enter_sem.at[t + 1, c, k, me],
            device_id=(section + 2 * c - 1, peer(step)),
            device_id_type=MESH,
        )

    def reduce_copy(c, t, k, step):
        return pltpu.make_async_remote_copy(
            src_ref=part.at[c, place(peer(step), k)],
            dst_ref=landed.at[t, c, step - 1, here(k)],
            send_sem=rs_send.at[t, c, k, step - 1],
            recv_sem=rs_recv.at[t, c, k, step - 1],
            device_id=(section, peer(step)),
            device_id_type=MESH,
        )

    def goes_on(c, t):
        target = section + 2 * c - 1
        return (target >= 0) & (target < sections) & (t + 1 < ticks)

    def begins(c, t):
        origin = section - 2 * c + 1
        return ((origin < 0) | (origin >= sections)) & (t + 1 < ticks)

    for c in range(2):
        for k in range(chunks):
            feed(arriving_ref.at[c, here(k)], c, 0, k)

    def finish(c, t, k):
        total = (
            entering[t, c, place(me, k), :].astype(jnp.float32)
            + part[c, place(me, k), :].astype(jnp.float32)
        )
        for step in range(1, group):
            copy = reduce_copy(c, t, k, step)
            copy.wait_send()
            copy.wait_recv()
            total += landed[t, c, step - 1, here(k), :].astype(jnp.float32)
        out_ref[c, t, here(k), :] = total.astype(jnp.bfloat16)

        @pl.when(goes_on(c, t))
        def _():
            for step in list(range(1, group)) + [0]:
                next_copy(c, t, k, step).start()

        @pl.when(begins(c, t))
        def _():
            feed(loss_ref.at[c, jnp.minimum(t, ticks - 2), here(k)], c, t + 1, k)

    tile = largest_divisor(inner, 768)
    heads = inner // HEAD
    unroll = largest_divisor(heads, 12)

    def doc_ids(lens, base, axis):
        places = lax.broadcasted_iota(jnp.int32, (seq, seq), axis)
        c, t = base
        first = lens[c, 0, t, 0]
        second = first + lens[c, 0, t, 1]
        third = second + lens[c, 0, t, 2]
        return (
            (places >= first).astype(jnp.int32)
            + (places >= second).astype(jnp.int32)
            + (places >= third).astype(jnp.int32)
        )

    def phase(index, carry):
        c = lax.rem(index, 2)
        t = index // 2
        for k in range(chunks):
            for source in range(group):
                pltpu.make_async_copy(
                    entering.at[t, c, place(source, k)],
                    entering.at[t, c, place(source, k)],
                    enter_sem.at[t, c, k, source],
                ).wait()

        @pl.when(t == 0)
        def _():
            load_wo(c).wait()

        def finish_before(low, high):
            @pl.when(index > 0)
            def _():
                before = jnp.maximum(index - 1, 0)
                for k in range(low, high):
                    finish(lax.rem(before, 2), before // 2, k)

        def out_tile(r, carry):
            span = pl.ds(pl.multiple_of(r * tile, tile), tile)
            attn[span, :] = jnp.dot(
                wo[c, span, :], entering[t, c], preferred_element_type=jnp.float32
            ).astype(jnp.bfloat16)
            return carry

        lax.fori_loop(0, inner // tile, out_tile, 0)
        for copy in load_qkv(c, t):
            copy.wait()
        base = (c, t)
        allowed = doc_ids(enc_ref, base, 0) == doc_ids(dec_ref, base, 1)

        def head_group(g, carry):
            for within in range(unroll):
                span = pl.ds(pl.multiple_of((g * unroll + within) * HEAD, HEAD), HEAD)
                key = ks[c, :, span]
                scores = lax.dot_general(
                    key, qs[c, :, span], (((1,), (1,)), ((), ())),
                    preferred_element_type=jnp.float32,
                ) * HEAD ** (-0.5)
                scores = jnp.where(allowed, scores, -1e30)
                top = jnp.max(scores, axis=0, keepdims=True)
                weights = jnp.exp(scores - top)
                weights = weights * (1.0 / jnp.sum(weights, axis=0, keepdims=True))
                prob_grad = jnp.dot(
                    vs[c, :, span], attn[span, :], preferred_element_type=jnp.float32
                )
                rowdot = jnp.sum(weights * prob_grad, axis=0, keepdims=True)
                score_grad = (weights * (prob_grad - rowdot)).astype(jnp.bfloat16)
                dqt[span, :] = (
                    lax.dot_general(
                        key, score_grad, (((0,), (0,)), ((), ())),
                        preferred_element_type=jnp.float32,
                    ) * HEAD ** (-0.5)
                ).astype(jnp.bfloat16)
            return carry

        finish_before(0, chunks // 2)
        lax.fori_loop(0, heads // unroll, head_group, 0)
        finish_before(chunks // 2, chunks)

        @pl.when(t + 1 < ticks)
        def _():
            for copy in load_qkv(c, jnp.minimum(t + 1, ticks - 1)):
                copy.start()

        @pl.when(t == 0)
        def _():
            load_wq(c).wait()

        def head_term(source, k):
            span = place(source, k)
            part[c, span, :] = jnp.dot(
                wq[c, span, :], dqt[...], preferred_element_type=jnp.float32
            ).astype(jnp.bfloat16)

        def send_chunk(k, carry):
            for step in range(1, group):
                head_term(peer(step), k)
                reduce_copy(c, t, k, step).start()
            return carry

        lax.fori_loop(0, chunks, send_chunk, 0)

        def own_chunk(k, carry):
            head_term(me, k)
            return carry

        lax.fori_loop(0, chunks, own_chunk, 0)
        return carry

    lax.fori_loop(0, 2 * ticks, phase, 0)

    def last_chunk(k, carry):
        finish(1, ticks - 1, k)
        return carry

    lax.fori_loop(0, chunks, last_chunk, 0)

    def drain(index, carry):
        c = lax.rem(index, 2)
        t = index // 2

        @pl.when(t == 0)
        def _():
            for k in range(chunks):
                for step in range(1, group):
                    feed_copy(arriving_ref.at[c, here(k)], c, 0, k, step).wait_send()

        @pl.when(goes_on(c, t))
        def _():
            for k in range(chunks):
                for step in range(group):
                    next_copy(c, t, k, step).wait_send()

        @pl.when(begins(c, t))
        def _():
            for k in range(chunks):
                for step in range(1, group):
                    feed_copy(
                        loss_ref.at[c, jnp.minimum(t, ticks - 2), here(k)], c, t + 1, k, step
                    ).wait_send()

        return carry

    lax.fori_loop(0, 2 * ticks, drain, 0)


def local(
    queries, enc_keys, enc_values, w_query, w_out, arriving, loss_grad, dec_lengths, enc_lengths
):
    sections = lax.axis_size("section")
    group = lax.axis_size("tensor")
    _, _, ticks, seq, inner = queries.shape
    width = w_query.shape[2]
    rows = arriving.shape[2]
    chunk = largest_divisor(rows, CHUNK)
    chunks = rows // chunk
    bf16 = jnp.bfloat16
    vmem = pl.BlockSpec(memory_space=pltpu.VMEM)
    smem = pl.BlockSpec(memory_space=pltpu.SMEM)
    anywhere = pl.BlockSpec(memory_space=pl.ANY)
    dma = pltpu.SemaphoreType.DMA
    grads = pl.pallas_call(
        functools.partial(
            relay_kernel, sections, group, (ticks, seq, inner, width, rows, chunk)
        ),
        out_shape=jax.ShapeDtypeStruct((2, ticks, rows, seq), bf16),
        in_specs=[smem, smem] + [anywhere] * 7,
        out_specs=vmem,
        scratch_shapes=[
            pltpu.VMEM((2, width, inner), bf16),
            pltpu.VMEM((2, inner, width), bf16),
            pltpu.VMEM((2, seq, inner), bf16),
            pltpu.VMEM((2, seq, inner), bf16),
            pltpu.VMEM((2, seq, inner), bf16),
            pltpu.VMEM((ticks, 2, width, seq), bf16),
            pltpu.VMEM((inner, seq), bf16),
            pltpu.VMEM((inner, seq), bf16),
            pltpu.VMEM((2, width, seq), bf16),
            pltpu.VMEM((ticks, 2, group - 1, rows, seq), bf16),
            dma((2,)),
            dma((2,)),
            dma((2, 3)),
            dma((ticks, 2, chunks, group)),
            dma((ticks, 2, chunks, group)),
            dma((ticks, 2, chunks, group)),
            dma((ticks, 2, chunks, group - 1)),
            dma((ticks, 2, chunks, group - 1)),
        ],
        compiler_params=pltpu.CompilerParams(
            collective_id=0, has_side_effects=True, vmem_limit_bytes=60 * 1024 * 1024
        ),
        cost_estimate=pl.CostEstimate(
            flops=4 * ticks * inner * (2 * width + 3 * seq) * seq,
            bytes_accessed=2 * (4 * width * inner + 6 * ticks * seq * inner),
            transcendentals=2 * ticks * seq * inner,
        ),
    )(
        dec_lengths,
        enc_lengths,
        queries[:, 0],
        enc_keys[:, 0],
        enc_values[:, 0],
        w_query[:, 0],
        w_out[:, 0],
        arriving[:, 0],
        loss_grad,
    )
    return grads[:, None]


def solution(mesh):
    in_specs = (
        P(None, "section", None, None, "tensor"),
        P(None, "section", None, None, "tensor"),
        P(None, "section", None, None, "tensor"),
        P(None, "section", None, "tensor"),
        P(None, "section", "tensor", None),
        P(None, "section", "tensor", None),
        P(None, None, "tensor", None),
        P(None, "section", None, None),
        P(None, "section", None, None),
    )
    out_specs = P(None, "section", None, "tensor", None)
    return jax.shard_map(local, mesh=mesh, in_specs=in_specs, out_specs=out_specs, check_vma=False)
```
